32 devices in a mesh: tm: 4 (over y, x), feed: 8 (over z, core).
Axes of the slice: x: 2, y: 2, z: 4, core: 2. Of those that a mesh axis runs over, the one named last changes fastest.
Arguments:
- voltages: bfloat16 [2048, 98304], P('feed', 'tm'), may hold values from -6 to 6
- gains: bfloat16 [2, 2048, 1024], P(None, 'feed'), may hold values from -4 to 4
- beam_weights: bfloat16 [2, 2048, 2048], replicated, may hold values from -0.09375 to 0.09375
- delay_filter: float32 [1024, 1024], replicated, may hold values from -0.21875 to 0.21875
- channel_lists: int32 [8, 192], replicated, may hold values from -1 to 1023, as said below
- beam_order: int32 [2048], replicated, may hold values from 0 to 2047, each once
Outputs:
- filtered: float32 [4, 2048, 1024], P('tm', 'feed')
The draws below stay inside these ranges and needn't reach their ends.
Inputs may be any that keep to these rules, and one draw needn't show every extreme that they name: `channel_lists`: each row holds distinct channel numbers in its first places and -1 in the rest; 768 channel numbers are listed in all, none twice; a row lists 0 to 192 channels, and some row lists exactly 192.
All inputs are finite; a program needn't handle non-finite values.
Results may differ from the reference program's by a relative error of at most 0.0021.
Values may be sent and summed in bfloat16 or wider, within the bound.
A program may use at most 192 MiB of HBM per device.

```python
import jax
import jax.numpy as jnp
from jax import lax

INPUTS = 2048
FFT = 2048
BEAMS = 2048
FR = 12
CHANNELS = 1024
LIVE = 768
SAMPLES = 98304
N_TM = 4
N_FEED = 8


def draw_channel_lists(key, part):
    even_share = LIVE // N_FEED
    capacity = 2 * even_share
    selected = jax.random.permutation(jax.random.fold_in(key, 11), CHANNELS)[:LIVE].astype(jnp.int32)
    shuffled = jax.random.permutation(jax.random.fold_in(key, 12), N_FEED).astype(jnp.int32)
    transfer = jax.random.randint(jax.random.fold_in(key, 13), (N_FEED // 2,), 0, even_share + 1).astype(jnp.int32)
    transfer = transfer.at[0].set(even_share)
    row_counts = jnp.full((N_FEED,), even_share, jnp.int32)
    row_counts = row_counts.at[shuffled[0::2]].add(transfer)
    row_counts = row_counts.at[shuffled[1::2]].add(-transfer)
    row_starts = jnp.cumsum(row_counts) - row_counts
    positions = jnp.arange(capacity, dtype=jnp.int32)[None, :]
    source_place = jnp.clip(row_starts[:, None] + positions, 0, LIVE - 1)
    return jnp.where(positions < row_counts[:, None], selected[source_place], -1).astype(jnp.int32)


def block_levels(key, extent, cuts, low, top_value):
    def one(dim, shards_of):
        draws = jax.random.uniform(jax.random.fold_in(jax.random.fold_in(key, 6), dim), (shards_of,), jnp.float32, low / len(cuts), top_value / len(cuts))
        return jnp.repeat(jnp.exp(draws), extent[dim] // shards_of).reshape((-1,) + (1,) * (len(extent) - dim - 1))

    gain = one(*cuts[0])
    for cut in cuts[1:]:
        gain = gain * one(*cut)
    return gain


def gaussian(rng, dims, scale, most, cuts=(), kind=jnp.bfloat16):
    factor_of = block_levels(rng, dims, cuts, -0.22, 0.18) if cuts else 1.0
    array = jax.random.normal(rng, dims, jnp.float32) * scale * factor_of
    return jnp.minimum(jnp.maximum(array, -most), most).astype(kind)


def setup_inputs(seed: int = 0) -> dict:
    splits = jax.random.split(jax.random.key(seed), 7)
    return {
        "voltages": gaussian(splits[0], (INPUTS, SAMPLES), 1.0, 6.0, ((0, 8), (1, 4))),
        "gains": gaussian(splits[1], (2, INPUTS, CHANNELS), 0.7, 4.0, ((1, 8),)),
        "beam_weights": gaussian(splits[2], (2, BEAMS, INPUTS), (2 * INPUTS) ** -0.5, 0.09375),
        "delay_filter": gaussian(splits[3], (CHANNELS, CHANNELS), LIVE ** -0.5, 0.21875, (), jnp.float32),
        "channel_lists": draw_channel_lists(jax.random.fold_in(splits[6], 71), 0),
        "beam_order": jax.random.permutation(splits[5], BEAMS).astype(jnp.int32),
    }


def make_window(length):
    places = jnp.arange(4 * length, dtype=jnp.float32)
    centred = (places - 2.0 * length + 0.5) / length
    taper = 0.5 - 0.5 * jnp.cos(2.0 * jnp.pi * (places + 0.5) / (4.0 * length))
    return (jnp.sinc(centred) * taper).reshape(4, length)


def make_table(length):
    sample_rows = jnp.arange(length, dtype=jnp.int32)[:, None]
    channel_cols = jnp.arange(length // 2, dtype=jnp.int32)[None, :]
    phases = ((sample_rows * channel_cols) % length).astype(jnp.float32)
    angles = 2.0 * jnp.pi * phases / length
    scaling = length ** -0.5
    return jnp.concatenate([jnp.cos(angles) * scaling, -jnp.sin(angles) * scaling], axis=1).astype(jnp.bfloat16)


def filterbank(extended, window, dft_table, frame_count):
    weighted = window[0] * extended[:, 0:frame_count].astype(jnp.float32)
    for tap_index in range(1, 4):
        weighted = weighted + window[tap_index] * extended[:, tap_index:tap_index + frame_count].astype(jnp.float32)
    weighted = weighted.astype(jnp.bfloat16)
    rows = weighted.shape[0] * frame_count
    flat_rows = weighted.reshape(rows, weighted.shape[2]).astype(jnp.float32)
    spectra = jnp.dot(flat_rows, dft_table.astype(jnp.float32), preferred_element_type=jnp.float32)
    return spectra.reshape(weighted.shape[0], frame_count, dft_table.shape[1])


def reference(voltages, gains, beam_weights, delay_filter, channel_lists, beam_order):
    window = make_window(FFT)
    dft_table = make_table(FFT)
    flattened = channel_lists.reshape(-1)
    listed = flattened >= 0
    safe_ids = jnp.where(listed, flattened, 0).astype(jnp.int32)
    live_mask = jnp.zeros((CHANNELS,), jnp.float32).at[safe_ids].add(listed.astype(jnp.float32))
    weights = beam_weights.reshape(2 * BEAMS, INPUTS).astype(jnp.float32)
    all_frames = voltages.reshape(INPUTS, N_TM, FR, FFT)
    gain_real = gains[0].astype(jnp.float32)[:, None, :]
    gain_imag = gains[1].astype(jnp.float32)[:, None, :]
    columns = CHANNELS * FR
    results = []
    for block_index in range(N_TM):
        if block_index == 0:
            earlier = jnp.zeros((INPUTS, 3, FFT), jnp.bfloat16)
        else:
            earlier = all_frames[:, block_index - 1, FR - 3:]
        extended = jnp.concatenate([earlier, all_frames[:, block_index]], axis=1)
        spectra = filterbank(extended, window, dft_table, FR)
        real_part = spectra[:, :, :CHANNELS]
        imag_part = spectra[:, :, CHANNELS:]
        gained_real = (real_part * gain_real - imag_part * gain_imag).astype(jnp.bfloat16)
        gained_imag = (real_part * gain_imag + imag_part * gain_real).astype(jnp.bfloat16)
        stacked = jnp.stack([gained_real, gained_imag], axis=1)
        stacked = jnp.transpose(stacked, (0, 1, 3, 2)).reshape(INPUTS, 2 * columns)
        product = jnp.dot(weights, stacked.astype(jnp.float32), preferred_element_type=jnp.float32)
        beams_real = product[:BEAMS, :columns] - product[BEAMS:, columns:]
        beams_imag = product[:BEAMS, columns:] + product[BEAMS:, :columns]
        powers = (beams_real * beams_real + beams_imag * beams_imag).reshape(BEAMS, CHANNELS, FR)
        powers = jnp.mean(powers, axis=2)
        masked = powers * live_mask[None, :]
        filtered = jnp.dot(masked, delay_filter, precision=lax.Precision.HIGHEST, preferred_element_type=jnp.float32)
        results.append(filtered[beam_order])
    return jnp.stack(results, axis=0)
```

```python
import functools

import jax
import jax.numpy as jnp
from jax import lax
from jax.experimental import pallas as pl
from jax.experimental.pallas import tpu as pltpu
from jax.sharding import PartitionSpec as P

FFT = 2048
CHANNELS = 1024
LIVE = 768
VMEM = 56 * 1024 * 1024
BF = jnp.bfloat16
F32 = jnp.float32
PARTS = ((3, 3), (6, 6), (0, 3))
NT = (((1,), (1,)), ((), ()))


def from_behind(block, axis, distance):
    devices = range(lax.axis_size(axis))
    route = [(i - distance, i) for i in devices if i - distance in devices]
    return lax.ppermute(block, axis, route)


def make_window(length):
    places = jnp.arange(4 * length, dtype=F32)
    centred = (places - 2.0 * length + 0.5) / length
    taper = 0.5 - 0.5 * jnp.cos(2.0 * jnp.pi * (places + 0.5) / (4.0 * length))
    return (jnp.sinc(centred) * taper).reshape(4, length)


def make_table(length):
    channel_rows = jnp.arange(length // 2, dtype=jnp.int32)[:, None]
    sample_cols = jnp.arange(length, dtype=jnp.int32)[None, :]
    phases = (channel_rows * sample_cols % length).astype(F32)
    angles = 2.0 * jnp.pi * phases / length
    scaling = length ** (-0.5)
    return (jnp.cos(angles) * scaling).astype(BF), (-jnp.sin(angles) * scaling).astype(BF)


def bank_kernel(groups, hist_ref, frame_ref, window_ref, table_ref, gain_ref, out_ref, past):
    step = pl.program_id(0)

    @pl.when(step == 0)
    def _():
        for t in range(3):
            past[t] = hist_ref[:, t * FFT : (t + 1) * FFT]

    now = frame_ref[...]
    total = window_ref[0:1, :] * past[lax.rem(step, 3)].astype(F32)
    total = total + window_ref[1:2, :] * past[lax.rem(step + 1, 3)].astype(F32)
    total = total + window_ref[2:3, :] * past[lax.rem(step + 2, 3)].astype(F32)
    total = total + window_ref[3:4, :] * now.astype(F32)
    past[lax.rem(step, 3)] = now
    weighted = total.astype(BF)
    slots = LIVE // groups
    for g in range(groups):
        rows = slice(g * slots, (g + 1) * slots)
        real = lax.dot_general(table_ref[0, rows, :], weighted, NT, preferred_element_type=F32)
        imag = lax.dot_general(table_ref[1, rows, :], weighted, NT, preferred_element_type=F32)
        gr = gain_ref[0, rows, :].astype(F32)
        gi = gain_ref[1, rows, :].astype(F32)
        out_ref[g, 0, 0] = (real * gr - imag * gi).astype(BF)
        out_ref[g, 1, 0] = (real * gi + imag * gr).astype(BF)


def bank(earlier, voltages, window, table, gain, groups, first, count):
    inputs = voltages.shape[0]
    slots = LIVE // groups
    hist = earlier if first == 0 else voltages
    place = 0 if first == 0 else first // 3 - 1
    return pl.pallas_call(
        functools.partial(bank_kernel, groups),
        grid=(count,),
        out_shape=jax.ShapeDtypeStruct((groups, 2, count, slots, inputs), BF),
        in_specs=[
            pl.BlockSpec((inputs, 3 * FFT), lambda k: (0, place)),
            pl.BlockSpec((inputs, FFT), lambda k: (0, first + k)),
            pl.BlockSpec((4, FFT), lambda k: (0, 0)),
            pl.BlockSpec((2, LIVE, FFT), lambda k: (0, 0, 0)),
            pl.BlockSpec((2, LIVE, inputs), lambda k: (0, 0, 0)),
        ],
        out_specs=pl.BlockSpec((groups, 2, 1, slots, inputs), lambda k: (0, 0, k, 0, 0)),
        scratch_shapes=[pltpu.VMEM((3, inputs, FFT), BF)],
        compiler_params=pltpu.CompilerParams(vmem_limit_bytes=VMEM),
        cost_estimate=pl.CostEstimate(
            flops=4 * count * inputs * FFT * LIVE,
            bytes_accessed=2 * count * inputs * (FFT + 2 * LIVE) + 4 * LIVE * FFT,
            transcendentals=0,
        ),
    )(hist, voltages, window, table, gain)


def beam_kernel(got_ref, weight_ref, before_ref, out_ref, held):
    groups, _, count, slots, inputs = got_ref.shape

    @pl.when(pl.program_id(0) == 0)
    def _():
        for g in range(groups):
            cols = slice(g * inputs, (g + 1) * inputs)
            real = got_ref[g, 0].reshape(count * slots, inputs)
            imag = got_ref[g, 1].reshape(count * slots, inputs)
            held[0, :, cols] = real
            held[1, :, cols] = imag
            held[2, :, cols] = (real.astype(F32) + imag.astype(F32)).astype(BF)

    wr, wi = weight_ref[0], weight_ref[1]
    less = (wi.astype(F32) - wr.astype(F32)).astype(BF)
    more = (wi.astype(F32) + wr.astype(F32)).astype(BF)
    both = lax.dot_general(held[2], wr, NT, preferred_element_type=F32)
    one = lax.dot_general(held[0], less, NT, preferred_element_type=F32)
    two = lax.dot_general(held[1], more, NT, preferred_element_type=F32)
    real, imag = both - two, both + one
    power = (real * real + imag * imag).reshape(count, slots, real.shape[1])
    out_ref[...] = before_ref[...] + jnp.sum(power, axis=0)


def beams(got, weights, before):
    groups, _, count, slots, inputs = got.shape
    total, deep = weights.shape[1:]
    tile = 256
    return pl.pallas_call(
        beam_kernel,
        grid=(total // tile,),
        out_shape=jax.ShapeDtypeStruct((slots, total), F32),
        in_specs=[
            pl.BlockSpec(got.shape, lambda b: (0, 0, 0, 0, 0)),
            pl.BlockSpec((2, tile, deep), lambda b: (0, b, 0)),
            pl.BlockSpec((slots, tile), lambda b: (0, b)),
        ],
        out_specs=pl.BlockSpec((slots, tile), lambda b: (0, b)),
        scratch_shapes=[pltpu.VMEM((3, count * slots, deep), BF)],
        compiler_params=pltpu.CompilerParams(vmem_limit_bytes=VMEM),
        cost_estimate=pl.CostEstimate(
            flops=6 * count * slots * deep * total,
            bytes_accessed=4 * total * deep + 4 * count * slots * deep,
            transcendentals=0,
        ),
    )(got, weights, before)


def plain_bank(earlier, voltages, window, table, gain, groups, first, count):
    inputs = voltages.shape[0]
    whole = jnp.concatenate([earlier, voltages], axis=1).reshape(inputs, -1, FFT)
    total = 0.0
    for t in range(4):
        total = total + window[t] * whole[:, first + t : first + t + count].astype(F32)
    spectra = jnp.einsum("rcn,ikn->rkci", table, total.astype(BF), preferred_element_type=F32)
    gr, gi = gain[0].astype(F32), gain[1].astype(F32)
    real, imag = spectra[0], spectra[1]
    gained = jnp.stack([real * gr - imag * gi, real * gi + imag * gr]).astype(BF)
    gained = gained.reshape(2, count, groups, LIVE // groups, inputs)
    return jnp.transpose(gained, (2, 0, 1, 3, 4))


def plain_beams(got, weights, before):
    groups, _, count, slots, inputs = got.shape
    flat = jnp.transpose(got, (1, 2, 3, 0, 4)).reshape(2, count * slots, groups * inputs)
    parts = jnp.einsum("xri,ybi->xyrb", flat, weights, preferred_element_type=F32)
    real, imag = parts[0, 0] - parts[1, 1], parts[0, 1] + parts[1, 0]
    power = (real * real + imag * imag).reshape(count, slots, -1)
    return before + jnp.sum(power, axis=0)


def body(voltages, gains, beam_weights, delay_filter, channel_lists, beam_order):
    groups = lax.axis_size("feed")
    inputs = voltages.shape[0]
    frames_here = voltages.shape[1] // FFT
    total_beams = beam_weights.shape[1]
    slots = LIVE // groups
    aligned = inputs % 128 == 0 and slots % 16 == 0
    run_bank, run_beams = (bank, beams) if aligned else (plain_bank, plain_beams)
    earlier = from_behind(voltages[:, (frames_here - 3) * FFT :], "tm", 1)
    window = make_window(FFT)

    numbers = jnp.arange(CHANNELS, dtype=jnp.int32)
    live = jnp.any(channel_lists.reshape(-1)[:, None] == numbers[None, :], axis=0)
    below = (numbers[:, None] < numbers[None, :]).astype(BF)
    rank = jnp.dot(live.astype(BF)[None, :], below, preferred_element_type=F32)[0]
    rank = rank.astype(jnp.int32)
    places = jnp.arange(LIVE, dtype=jnp.int32)[:, None]
    pick = ((rank[None, :] == places) & live[None, :]).astype(BF)

    cosines, sines = make_table(FFT)
    table = jnp.stack([jnp.dot(pick, cosines), jnp.dot(pick, sines)])
    gain = jnp.einsum("sc,ric->rsi", pick, gains)
    rows = jnp.dot(pick.astype(F32), delay_filter, precision=lax.Precision.HIGHEST)
    order = (beam_order[None, :] == jnp.arange(total_beams, dtype=jnp.int32)[:, None]).astype(BF)

    powers = jnp.zeros((slots, total_beams), F32)
    outgoing = [
        run_bank(earlier, voltages, window, table, gain, groups, first, count)
        for first, count in PARTS
    ]
    for block in outgoing:
        got = lax.all_to_all(block, "feed", split_axis=0, concat_axis=0, tiled=True)
        powers = run_beams(got, beam_weights, powers)
    powers = (powers * (1.0 / frames_here)).astype(BF)
    ordered = jnp.dot(powers, order, preferred_element_type=F32).astype(BF)
    ordered = jnp.transpose(ordered.reshape(slots, groups, total_beams // groups), (1, 0, 2))
    owned = lax.all_to_all(ordered, "feed", split_axis=0, concat_axis=0, tiled=True)
    owned = owned.reshape(LIVE, total_beams // groups).astype(F32)
    filtered = lax.dot_general(
        owned, rows, (((0,), (0,)), ((), ())), precision=lax.Precision.HIGHEST,
        preferred_element_type=F32,
    )
    return filtered[None]


def solution(mesh):
    placed = (P("feed", "tm"), P(None, "feed", None), P(), P(), P(), P())
    return jax.shard_map(
        body, mesh=mesh, in_specs=placed, out_specs=P("tm", "feed", None), check_vma=False
    )
```

```python
import functools

import jax
import jax.numpy as jnp
import numpy as np
from jax import lax
from jax.experimental import pallas as pl
from jax.experimental.pallas import tpu as pltpu
from jax.sharding import PartitionSpec as P

FFT = 2048
CHANNELS = 1024
LIVE = 768
VMEM = 56 * 1024 * 1024
BF = jnp.bfloat16
F32 = jnp.float32
PARTS = ((3, 3), (6, 6), (0, 3))
NT = (((1,), (1,)), ((), ()))


def from_behind(block, axis, distance):
    devices = range(lax.axis_size(axis))
    route = [(i - distance, i) for i in devices if i - distance in devices]
    return lax.ppermute(block, axis, route)


def make_window(length):
    places = jnp.arange(4 * length, dtype=F32)
    centred = (places - 2.0 * length + 0.5) / length
    taper = 0.5 - 0.5 * jnp.cos(2.0 * jnp.pi * (places + 0.5) / (4.0 * length))
    return (jnp.sinc(centred) * taper).reshape(4, length)


def make_table(length):
    channel_rows = np.arange(length // 2, dtype=np.int32)[:, None]
    sample_cols = np.arange(length, dtype=np.int32)[None, :]
    phases = (channel_rows * sample_cols % length).astype(np.float32)
    angles = np.float32(2.0 * np.pi) * phases / np.float32(length)
    scaling = np.float32(length ** (-0.5))
    return np.stack([np.cos(angles) * scaling, -np.sin(angles) * scaling]).astype(BF)


def bank_kernel(groups, hist_ref, frame_ref, window_ref, table_ref, gain_ref, out_ref, past):
    step = pl.program_id(0)

    @pl.when(step == 0)
    def _():
        for t in range(3):
            past[t] = hist_ref[:, t * FFT : (t + 1) * FFT]

    now = frame_ref[...]
    total = window_ref[0:1, :] * past[lax.rem(step, 3)].astype(F32)
    total = total + window_ref[1:2, :] * past[lax.rem(step + 1, 3)].astype(F32)
    total = total + window_ref[2:3, :] * past[lax.rem(step + 2, 3)].astype(F32)
    total = total + window_ref[3:4, :] * now.astype(F32)
    past[lax.rem(step, 3)] = now
    weighted = total.astype(BF)
    table = table_ref[...].reshape(2 * LIVE, FFT)
    spectra = lax.dot_general(table, weighted, NT, preferred_element_type=F32)
    real, imag = spectra[:LIVE], spectra[LIVE:]
    gr = gain_ref[0].astype(F32)
    gi = gain_ref[1].astype(F32)
    gained_real = (real * gr - imag * gi).astype(BF)
    gained_imag = (real * gi + imag * gr).astype(BF)
    slots = LIVE // groups
    for g in range(groups):
        out_ref[g, 0, 0] = gained_real[g * slots : (g + 1) * slots]
        out_ref[g, 1, 0] = gained_imag[g * slots : (g + 1) * slots]


def bank(earlier, voltages, window, table, gain, groups, first, count):
    inputs = voltages.shape[0]
    slots = LIVE // groups
    hist = earlier if first == 0 else voltages
    place = 0 if first == 0 else first // 3 - 1
    return pl.pallas_call(
        functools.partial(bank_kernel, groups),
        grid=(count,),
        out_shape=jax.ShapeDtypeStruct((groups, 2, count, slots, inputs), BF),
        in_specs=[
            pl.BlockSpec((inputs, 3 * FFT), lambda k: (0, place)),
            pl.BlockSpec((inputs, FFT), lambda k: (0, first + k)),
            pl.BlockSpec((4, FFT), lambda k: (0, 0)),
            pl.BlockSpec((2, LIVE, FFT), lambda k: (0, 0, 0)),
            pl.BlockSpec((2, LIVE, inputs), lambda k: (0, 0, 0)),
        ],
        out_specs=pl.BlockSpec((groups, 2, 1, slots, inputs), lambda k: (0, 0, k, 0, 0)),
        scratch_shapes=[pltpu.VMEM((3, inputs, FFT), BF)],
        compiler_params=pltpu.CompilerParams(vmem_limit_bytes=VMEM),
        cost_estimate=pl.CostEstimate(
            flops=4 * count * inputs * FFT * LIVE,
            bytes_accessed=2 * count * inputs * (FFT + 2 * LIVE) + 4 * LIVE * FFT,
            transcendentals=0,
        ),
    )(hist, voltages, window, table, gain)


def beam_kernel(got_ref, weight_ref, before_ref, out_ref, held):
    groups, _, count, slots, inputs = got_ref.shape
    rows = count * slots

    @pl.when(pl.program_id(0) == 0)
    def _():
        for g in range(groups):
            cols = slice(g * inputs, (g + 1) * inputs)
            held[:, cols] = got_ref[g].reshape(2 * rows, inputs)

    by_real = lax.dot_general(held[...], weight_ref[0], NT, preferred_element_type=F32)
    by_imag = lax.dot_general(held[...], weight_ref[1], NT, preferred_element_type=F32)
    real = by_real[:rows] - by_imag[rows:]
    imag = by_real[rows:] + by_imag[:rows]
    power = (real * real + imag * imag).reshape(count, slots, real.shape[1])
    out_ref[...] = before_ref[...] + jnp.sum(power, axis=0)


def beams(got, weights, before):
    groups, _, count, slots, inputs = got.shape
    total, deep = weights.shape[1:]
    tile = 256
    return pl.pallas_call(
        beam_kernel,
        grid=(total // tile,),
        out_shape=jax.ShapeDtypeStruct((slots, total), F32),
        in_specs=[
            pl.BlockSpec(got.shape, lambda b: (0, 0, 0, 0, 0)),
            pl.BlockSpec((2, tile, deep), lambda b: (0, b, 0)),
            pl.BlockSpec((slots, tile), lambda b: (0, b)),
        ],
        out_specs=pl.BlockSpec((slots, tile), lambda b: (0, b)),
        scratch_shapes=[pltpu.VMEM((2 * count * slots, deep), BF)],
        compiler_params=pltpu.CompilerParams(vmem_limit_bytes=VMEM),
        cost_estimate=pl.CostEstimate(
            flops=8 * count * slots * deep * total,
            bytes_accessed=4 * total * deep + 4 * count * slots * deep,
            transcendentals=0,
        ),
    )(got, weights, before)


def plain_bank(earlier, voltages, window, table, gain, groups, first, count):
    inputs = voltages.shape[0]
    whole = jnp.concatenate([earlier, voltages], axis=1).reshape(inputs, -1, FFT)
    total = 0.0
    for t in range(4):
        total = total + window[t] * whole[:, first + t : first + t + count].astype(F32)
    spectra = jnp.einsum("rcn,ikn->rkci", table, total.astype(BF), preferred_element_type=F32)
    gr, gi = gain[0].astype(F32), gain[1].astype(F32)
    real, imag = spectra[0], spectra[1]
    gained = jnp.stack([real * gr - imag * gi, real * gi + imag * gr]).astype(BF)
    gained = gained.reshape(2, count, groups, LIVE // groups, inputs)
    return jnp.transpose(gained, (2, 0, 1, 3, 4))


def plain_beams(got, weights, before):
    groups, _, count, slots, inputs = got.shape
    flat = jnp.transpose(got, (1, 2, 3, 0, 4)).reshape(2, count * slots, groups * inputs)
    parts = jnp.einsum("xri,ybi->xyrb", flat, weights, preferred_element_type=F32)
    real, imag = parts[0, 0] - parts[1, 1], parts[0, 1] + parts[1, 0]
    power = (real * real + imag * imag).reshape(count, slots, -1)
    return before + jnp.sum(power, axis=0)


def body(voltages, gains, beam_weights, delay_filter, channel_lists, beam_order):
    groups = lax.axis_size("feed")
    inputs = voltages.shape[0]
    frames_here = voltages.shape[1] // FFT
    total_beams = beam_weights.shape[1]
    slots = LIVE // groups
    aligned = inputs % 128 == 0 and slots % 16 == 0
    run_bank, run_beams = (bank, beams) if aligned else (plain_bank, plain_beams)
    earlier = from_behind(voltages[:, (frames_here - 3) * FFT :], "tm", 1)
    window = make_window(FFT)

    numbers = jnp.arange(CHANNELS, dtype=jnp.int32)
    live = jnp.any(channel_lists.reshape(-1)[:, None] == numbers[None, :], axis=0)
    below = (numbers[:, None] < numbers[None, :]).astype(BF)
    rank = jnp.dot(live.astype(BF)[None, :], below, preferred_element_type=F32)[0]
    rank = rank.astype(jnp.int32)
    places = jnp.arange(LIVE, dtype=jnp.int32)[:, None]
    pick = ((rank[None, :] == places) & live[None, :]).astype(BF)

    table = jnp.einsum("sc,rcn->rsn", pick, jnp.asarray(make_table(FFT)))
    gain = jnp.einsum("sc,ric->rsi", pick, gains)
    rows = jnp.dot(pick.astype(F32), delay_filter, precision=lax.Precision.HIGHEST)
    order = (beam_order[None, :] == jnp.arange(total_beams, dtype=jnp.int32)[:, None]).astype(BF)

    powers = jnp.zeros((slots, total_beams), F32)
    outgoing = [
        run_bank(earlier, voltages, window, table, gain, groups, first, count)
        for first, count in PARTS
    ]
    for at, block in enumerate(outgoing):
        got = lax.all_to_all(block, "feed", split_axis=0, concat_axis=0, tiled=True)
        if at == len(outgoing) - 1:
            powers, rows = lax.optimization_barrier((powers, rows))
        powers = run_beams(got, beam_weights, powers)
    powers = powers * (1.0 / frames_here)
    high = powers.astype(BF)
    low = (powers - high.astype(F32)).astype(BF)
    ordered = jnp.dot(jnp.concatenate([high, low], axis=0), order, preferred_element_type=F32)
    ordered = ordered[:slots] + ordered[slots:]
    ordered = jnp.transpose(ordered.reshape(slots, groups, total_beams // groups), (1, 0, 2))
    owned = lax.all_to_all(ordered, "feed", split_axis=0, concat_axis=0, tiled=True)
    owned = owned.reshape(LIVE, total_beams // groups)
    filtered = lax.dot_general(
        owned, rows, (((0,), (0,)), ((), ())), precision=lax.Precision.HIGHEST,
        preferred_element_type=F32,
    )
    return filtered[None]


def solution(mesh):
    placed = (P("feed", "tm"), P(None, "feed", None), P(), P(), P(), P())
    return jax.shard_map(
        body, mesh=mesh, in_specs=placed, out_specs=P("tm", "feed", None), check_vma=False
    )
```

```python
import functools

import jax
import jax.numpy as jnp
import numpy as np
from jax import lax
from jax.experimental import pallas as pl
from jax.experimental.pallas import tpu as pltpu
from jax.sharding import PartitionSpec as P

FFT = 2048
CHANNELS = 1024
LIVE = 768
VMEM = 56 * 1024 * 1024
BF = jnp.bfloat16
F32 = jnp.float32
PARTS = ((3, 3), (6, 6), (0, 3))
NT = (((1,), (1,)), ((), ()))


def from_behind(block, axis, distance):
    devices = range(lax.axis_size(axis))
    route = [(i - distance, i) for i in devices if i - distance in devices]
    return lax.ppermute(block, axis, route)


def make_window(length):
    places = jnp.arange(4 * length, dtype=F32)
    centred = (places - 2.0 * length + 0.5) / length
    taper = 0.5 - 0.5 * jnp.cos(2.0 * jnp.pi * (places + 0.5) / (4.0 * length))
    return (jnp.sinc(centred) * taper).reshape(4, length)


def make_table(length):
    channel_rows = np.arange(length // 2, dtype=np.int32)[:, None]
    sample_cols = np.arange(length, dtype=np.int32)[None, :]
    phases = (channel_rows * sample_cols % length).astype(np.float32)
    angles = np.float32(2.0 * np.pi) * phases / np.float32(length)
    scaling = np.float32(length ** (-0.5))
    return np.stack([np.cos(angles) * scaling, -np.sin(angles) * scaling]).astype(BF)


def bank_kernel(groups, hist_ref, frame_ref, window_ref, table_ref, gain_ref, out_ref, past):
    step = pl.program_id(0)

    @pl.when(step == 0)
    def _():
        for t in range(3):
            past[t] = hist_ref[:, t * FFT : (t + 1) * FFT]

    now = frame_ref[...]
    total = window_ref[0:1, :] * past[lax.rem(step, 3)].astype(F32)
    total = total + window_ref[1:2, :] * past[lax.rem(step + 1, 3)].astype(F32)
    total = total + window_ref[2:3, :] * past[lax.rem(step + 2, 3)].astype(F32)
    total = total + window_ref[3:4, :] * now.astype(F32)
    past[lax.rem(step, 3)] = now
    weighted = total.astype(BF)
    table = table_ref[...].reshape(2 * LIVE, FFT)
    spectra = lax.dot_general(table, weighted, NT, preferred_element_type=F32)
    real, imag = spectra[:LIVE], spectra[LIVE:]
    gr = gain_ref[0].astype(F32)
    gi = gain_ref[1].astype(F32)
    gained_real = (real * gr - imag * gi).astype(BF)
    gained_imag = (real * gi + imag * gr).astype(BF)
    slots = LIVE // groups
    for g in range(groups):
        out_ref[g, 0, 0] = gained_real[g * slots : (g + 1) * slots]
        out_ref[g, 1, 0] = gained_imag[g * slots : (g + 1) * slots]


def bank(earlier, voltages, window, table, gain, groups, first, count):
    inputs = voltages.shape[0]
    slots = LIVE // groups
    hist = earlier if first == 0 else voltages
    place = 0 if first == 0 else first // 3 - 1
    return pl.pallas_call(
        functools.partial(bank_kernel, groups),
        grid=(count,),
        out_shape=jax.ShapeDtypeStruct((groups, 2, count, slots, inputs), BF),
        in_specs=[
            pl.BlockSpec((inputs, 3 * FFT), lambda k: (0, place)),
            pl.BlockSpec((inputs, FFT), lambda k: (0, first + k)),
            pl.BlockSpec((4, FFT), lambda k: (0, 0)),
            pl.BlockSpec((2, LIVE, FFT), lambda k: (0, 0, 0)),
            pl.BlockSpec((2, LIVE, inputs), lambda k: (0, 0, 0)),
        ],
        out_specs=pl.BlockSpec((groups, 2, 1, slots, inputs), lambda k: (0, 0, k, 0, 0)),
        scratch_shapes=[pltpu.VMEM((3, inputs, FFT), BF)],
        compiler_params=pltpu.CompilerParams(vmem_limit_bytes=VMEM),
        cost_estimate=pl.CostEstimate(
            flops=4 * count * inputs * FFT * LIVE,
            bytes_accessed=2 * count * inputs * (FFT + 2 * LIVE) + 4 * LIVE * FFT,
            transcendentals=0,
        ),
    )(hist, voltages, window, table, gain)


def beam_kernel(got_ref, weight_ref, before_ref, out_ref, held):
    groups, _, count, slots, inputs = got_ref.shape
    rows = count * slots

    @pl.when(pl.program_id(0) == 0)
    def _():
        for g in range(groups):
            cols = slice(g * inputs, (g + 1) * inputs)
            held[:, cols] = got_ref[g].reshape(2 * rows, inputs)

    by_real = lax.dot_general(held[...], weight_ref[0], NT, preferred_element_type=F32)
    by_imag = lax.dot_general(held[...], weight_ref[1], NT, preferred_element_type=F32)
    real = by_real[:rows] - by_imag[rows:]
    imag = by_real[rows:] + by_imag[:rows]
    power = (real * real + imag * imag).reshape(count, slots, real.shape[1])
    out_ref[...] = before_ref[...] + jnp.sum(power, axis=0)


def beams(got, weights, before):
    groups, _, count, slots, inputs = got.shape
    total, deep = weights.shape[1:]
    tile = 256
    return pl.pallas_call(
        beam_kernel,
        grid=(total // tile,),
        out_shape=jax.ShapeDtypeStruct((slots, total), F32),
        in_specs=[
            pl.BlockSpec(got.shape, lambda b: (0, 0, 0, 0, 0)),
            pl.BlockSpec((2, tile, deep), lambda b: (0, b, 0)),
            pl.BlockSpec((slots, tile), lambda b: (0, b)),
        ],
        out_specs=pl.BlockSpec((slots, tile), lambda b: (0, b)),
        scratch_shapes=[pltpu.VMEM((2 * count * slots, deep), BF)],
        compiler_params=pltpu.CompilerParams(vmem_limit_bytes=VMEM),
        cost_estimate=pl.CostEstimate(
            flops=8 * count * slots * deep * total,
            bytes_accessed=4 * total * deep + 4 * count * slots * deep,
            transcendentals=0,
        ),
    )(got, weights, before)


def plain_bank(earlier, voltages, window, table, gain, groups, first, count):
    inputs = voltages.shape[0]
    whole = jnp.concatenate([earlier, voltages], axis=1).reshape(inputs, -1, FFT)
    total = 0.0
    for t in range(4):
        total = total + window[t] * whole[:, first + t : first + t + count].astype(F32)
    spectra = jnp.einsum("rcn,ikn->rkci", table, total.astype(BF), preferred_element_type=F32)
    gr, gi = gain[0].astype(F32), gain[1].astype(F32)
    real, imag = spectra[0], spectra[1]
    gained = jnp.stack([real * gr - imag * gi, real * gi + imag * gr]).astype(BF)
    gained = gained.reshape(2, count, groups, LIVE // groups, inputs)
    return jnp.transpose(gained, (2, 0, 1, 3, 4))


def plain_beams(got, weights, before):
    groups, _, count, slots, inputs = got.shape
    flat = jnp.transpose(got, (1, 2, 3, 0, 4)).reshape(2, count * slots, groups * inputs)
    parts = jnp.einsum("xri,ybi->xyrb", flat, weights, preferred_element_type=F32)
    real, imag = parts[0, 0] - parts[1, 1], parts[0, 1] + parts[1, 0]
    power = (real * real + imag * imag).reshape(count, slots, -1)
    return before + jnp.sum(power, axis=0)


def body(voltages, gains, beam_weights, delay_filter, channel_lists, beam_order):
    groups = lax.axis_size("feed")
    inputs = voltages.shape[0]
    frames_here = voltages.shape[1] // FFT
    total_beams = beam_weights.shape[1]
    slots = LIVE // groups
    aligned = inputs % 128 == 0 and slots % 16 == 0
    run_bank, run_beams = (bank, beams) if aligned else (plain_bank, plain_beams)
    earlier = from_behind(voltages[:, (frames_here - 3) * FFT :], "tm", 1)
    window = make_window(FFT)

    numbers = jnp.arange(CHANNELS, dtype=jnp.int32)
    live = jnp.any(channel_lists.reshape(-1)[:, None] == numbers[None, :], axis=0)
    below = (numbers[:, None] < numbers[None, :]).astype(BF)
    rank = jnp.dot(live.astype(BF)[None, :], below, preferred_element_type=F32)[0]
    rank = rank.astype(jnp.int32)
    places = jnp.arange(LIVE, dtype=jnp.int32)[:, None]
    pick = ((rank[None, :] == places) & live[None, :]).astype(BF)

    table = jnp.einsum("sc,rcn->rsn", pick, jnp.asarray(make_table(FFT)))
    gain = jnp.einsum("sc,ric->rsi", pick, gains)
    rows = jnp.dot(pick.astype(F32), delay_filter, precision=lax.Precision.HIGHEST)
    order = (beam_order[None, :] == jnp.arange(total_beams, dtype=jnp.int32)[:, None]).astype(BF)

    def exchange(block):
        return lax.all_to_all(block, "feed", split_axis=0, concat_axis=0, tiled=True)

    def by_owner(ordered):
        return jnp.transpose(ordered.reshape(slots, groups, total_beams // groups), (1, 0, 2))

    none = jnp.zeros((slots, total_beams), F32)
    powers = none
    for at, (first, count) in enumerate(PARTS):
        if at == len(PARTS) - 1:
            earlier, powers = lax.optimization_barrier((earlier, powers))
        block = run_bank(earlier, voltages, window, table, gain, groups, first, count)
        got = exchange(block)
        if at == len(PARTS) - 1:
            break
        if at:
            waiting = got
        else:
            powers = run_beams(got, beam_weights, powers)
    powers = run_beams(waiting, beam_weights, powers)
    powers, rows = lax.optimization_barrier((powers * (1.0 / frames_here), rows))
    high = lax.reduce_precision(powers, 8, 7)
    pair = jnp.concatenate([high.astype(BF), (powers - high).astype(BF)], axis=0)
    ordered = jnp.dot(pair, order, preferred_element_type=F32)
    ordered = by_owner(ordered[:slots] + ordered[slots:])
    got, ordered = lax.optimization_barrier((got, ordered))
    owned = exchange(ordered)
    last = (run_beams(got, beam_weights, none) * (1.0 / frames_here)).astype(BF)
    last = by_owner(jnp.dot(last, order, preferred_element_type=F32).astype(BF))
    owned, last = lax.optimization_barrier((owned, last))
    last = exchange(last)
    owned = (owned + last.astype(F32)).reshape(LIVE, total_beams // groups)
    filtered = lax.dot_general(
        owned, rows, (((0,), (0,)), ((), ())), precision=lax.Precision.HIGHEST,
        preferred_element_type=F32,
    )
    return filtered[None]


def solution(mesh):
    placed = (P("feed", "tm"), P(None, "feed", None), P(), P(), P(), P())
    return jax.shard_map(
        body, mesh=mesh, in_specs=placed, out_specs=P("tm", "feed", None), check_vma=False
    )
```
